256 devices in a mesh: dom: 32 (over x_hi, z, core), sub: 8 (over x_lo, y).
Axes of the slice: x: 4 (x_hi: 2, x_lo: 2; x = x_hi * 2 + x_lo), y: 4, z: 8, core: 2. Of those that a mesh axis runs over, the one named last changes fastest.
Arguments:
- particles: float32 [3072, 4096], P('dom', 'sub'), may hold values from -6 to 6
- gradient: float32 [3072, 4096], P('dom', 'sub'), may hold values from -0.012 to 0.012
- curvature: float32 [4096], P('sub'), may hold values from 0.0005 to 0.004
Outputs:
- moved: float32 [3072, 4096], P('dom', 'sub')
The draws below stay inside these ranges and needn't reach their ends.
All inputs are finite; a program needn't handle non-finite values.
Results may differ from the reference program's by a relative error of at most 0.000051.
Values sent between devices are 32-bit elements; how exact they have to be, the bound alone decides.
A program may use at most 64 MiB of HBM per device.

```python
import math
import jax
import jax.numpy as jnp
from jax import lax

RANK = 4096
PARTICLES = 3072


def level_of(rng, dims, pieces, low, top_value):
    gain, own = 1.0, jax.random.fold_in(rng, 6)
    for axis_at, parts in pieces:
        draws = jnp.exp(jax.random.uniform(jax.random.fold_in(own, axis_at), (parts,), jnp.float32, low / len(pieces), top_value / len(pieces)))
        gain = gain * jnp.repeat(draws, dims[axis_at] // parts).reshape([-1 if axis == axis_at else 1 for axis in range(len(dims))])
    return gain


def normal_values(key, dims, scale, limit, split=(), dtype=jnp.bfloat16):
    entries = jax.random.normal(key, dims, jnp.float32) * scale
    if len(split) > 0:
        entries = level_of(key, dims, split, -0.22, 0.18) * entries
    return jnp.clip(entries, min=-limit, max=limit).astype(dtype)


def setup_inputs(seed: int = 0) -> dict:
    arg_keys = jax.random.split(jax.random.key(seed), 4)
    particles = normal_values(arg_keys[0], (PARTICLES, RANK), 1.0, 6.0, ((0, 32), (1, 8)), jnp.float32)
    gradient = normal_values(arg_keys[1], (PARTICLES, RANK), 0.002, 0.012, ((0, 32), (1, 8)), jnp.float32)
    curvature = jnp.clip(jnp.exp(math.log(0.004) - 2.0794415 * jax.random.uniform(arg_keys[2], (RANK,), jnp.float32) ** level_of(arg_keys[2], (RANK,), ((0, 8),), -0.2, 0.2)), 0.0005, 0.004)
    return dict(particles=particles, gradient=gradient, curvature=curvature)


def stein_step(coords, grads):
    count = coords.shape[0]
    first = jnp.sum(coords, axis=0)
    second = jnp.sum(coords * coords)
    width = (2.0 * count * second - 2.0 * jnp.sum(first * first)) / (count * (count - 1.0)) / jnp.log(count + 1.0)
    norms = jnp.sum(coords * coords, axis=1)
    inner = jnp.dot(coords, coords.T, precision=lax.Precision.HIGHEST, preferred_element_type=jnp.float32)
    dist = norms[:, None] + norms[None, :] - 2.0 * inner
    kernel = jnp.exp(-dist / width)
    total = jnp.sum(kernel, axis=1)
    target = 0.5 * width * grads - coords
    pulled = jnp.dot(kernel, target, precision=lax.Precision.HIGHEST, preferred_element_type=jnp.float32)
    return 2.0 * coords + pulled / total[:, None]


def reference(particles, gradient, curvature):
    first_step = stein_step(particles, gradient)
    relinear = gradient - curvature[None, :] * (first_step - particles)
    return stein_step(first_step, relinear)
```

```python
import functools
import math

import jax
import jax.numpy as jnp
from jax import lax
from jax.experimental import pallas as pl
from jax.experimental.pallas import tpu as pltpu
from jax.sharding import PartitionSpec as P

F32, BF16 = jnp.float32, jnp.bfloat16
MESH = pl.DeviceIdType.MESH
NT = (((1,), (1,)), ((), ()))
TN = (((0,), (0,)), ((), ()))

GROUPS = ((1, 7), (2, 6), (3, 5), (0, 4))
SUBS = tuple((dx, dy) for dx in range(2) for dy in range(4))[1:]
CHUNKS = 4


def split(a):
    high = a.astype(BF16)
    return high, (a - high.astype(F32)).astype(BF16)


def dot3(a, b, dims):
    (ah, al), (bh, bl) = a, b
    dot = functools.partial(lax.dot_general, dimension_numbers=dims, preferred_element_type=F32)
    return dot(al, bh) + dot(ah, bl) + dot(ah, bh)


def copy_to(src, dst, send, recv, device):
    return pltpu.make_async_remote_copy(
        src_ref=src, dst_ref=dst, send_sem=send, recv_sem=recv, device_id=device, device_id_type=MESH
    )


def wait_bytes(ref, sem):
    pltpu.make_async_copy(ref, ref, sem).wait()


class Ring:
    def __init__(self, own, held, send, recv, right, left, by_columns):
        self.own, self.held, self.send, self.recv = own, held, send, recv
        self.to = (right, left)
        self.by_columns = by_columns

    def piece(self, d, chunk):
        ref = self.own if d == 0 else self.held.at[d]
        rows, columns = ref.shape
        if self.by_columns:
            width = columns // CHUNKS
            return ref.at[:, pl.ds(chunk * width, width)]
        height = rows // CHUNKS
        return ref.at[pl.ds(chunk * height, height)]

    def has(self, way, step, chunk):
        return step < 3 or (step == 3 and (chunk % 2 == way))

    def copy(self, way, step, chunk):
        src = (-step) % 8 if way == 0 else step
        dst = (-step - 1) % 8 if way == 0 else step + 1
        return copy_to(
            self.piece(src, chunk), self.piece(dst, chunk), self.send.at[way, step], self.recv.at[way, step, chunk],
            self.to[way],
        )

    def advance(self, step, chunk):
        for way in range(2):
            if step > 0 and self.has(way, step - 1, chunk):
                self.copy(way, step - 1, chunk).wait_recv()
            if self.has(way, step, chunk):
                self.copy(way, step, chunk).start()

    def drain(self):
        for way in range(2):
            for step in range(4):
                ref = self.own if step < 3 else self.own.at[pl.ds(0, self.own.shape[0] // 2)]
                wait_bytes(ref, self.send.at[way, step])


def kernel(
    x_ref, g_ref, c_ref, o_ref,
    x1_ref, held0, held1, heldg, xj, jh, jl, part, dist, rs_recv, kh, kl, th, tl,
    sums, sums_recv, scal, scal_recv, pull, sib_recv, half_send, half_recv,
    ring_send, ring_recv, xj_send, xj_recv, rs_ssem, rs_rsem, ag_ssem, ag_rsem,
    s_ssem, s_rsem, p_ssem, p_rsem,
):
    rows, cols = x_ref.shape
    dom, sub = lax.axis_index("dom"), lax.axis_index("sub")
    core, z, half = dom % 2, (dom // 2) % 8, dom // 16
    y, pair = sub % 4, sub // 4
    count = 1.0 * rows * lax.axis_size("dom")
    piece = 2 * rows // 8
    mine = pl.ds(pl.multiple_of(sub * piece, 8), piece)

    def at(dh, dz, dc):
        return (((half + dh) % 2 * 8 + (z + dz) % 8) * 2 + (core + dc) % 2, sub)

    def sub_index(dx, dy):
        return (pair + dx) % 2 * 4 + (y + dy) % 4

    right, left, sibling, other, cross = at(0, 1, 0), at(0, 7, 0), at(0, 0, 1), at(1, 0, 0), at(1, 0, 1)
    subs = [(dom, sub_index(dx, dy)) for dx, dy in SUBS]

    barrier = pltpu.get_barrier_semaphore()
    partners = [right, left, sibling, other, cross] + subs
    for partner in partners:
        pl.semaphore_signal(barrier, inc=1, device_id=partner, device_id_type=MESH)
    pl.semaphore_wait(barrier, len(partners))

    ring_g = Ring(g_ref, heldg, ring_send.at[2], ring_recv.at[2], right, left, True)

    def stein(s, own, held, make_target, out):
        ring = Ring(own, held, ring_send.at[s], ring_recv.at[s], right, left, False)

        def block(d):
            return own[...] if d == 0 else held[d]

        def xj_copy(k, chunk):
            rows_of = pl.ds(chunk * (rows // 2), rows // 2)
            src = own if k < 3 else xj.at[s, 2]
            return copy_to(
                src.at[rows_of], xj.at[s, k, rows_of], xj_send.at[s, k, chunk], xj_recv.at[s, k, chunk],
                other if k == 2 else sibling,
            )

        for chunk in range(2):
            xj_copy(2, chunk).start()
        for chunk in range(CHUNKS):
            ring.advance(0, chunk)
        for chunk in range(2):
            xj_copy(1, chunk).start()
        for chunk in range(CHUNKS):
            ring.advance(1, chunk)

        for chunk in range(2):
            xj_copy(2, chunk).wait_recv()
            xj_copy(3, chunk).start()
        xj[s, 0] = own[...]
        for chunk in range(2):
            xj_copy(1, chunk).wait_recv()
        for chunk in range(2):
            xj_copy(3, chunk).wait_recv()
        js = xj[s].reshape(4 * rows, cols)
        jh[...], jl[...] = split(-2.0 * js)
        norms_j = lax.dot_general(
            jnp.ones((8, cols), F32), js * js, NT, precision=lax.Precision.HIGHEST, preferred_element_type=F32
        )[0:1]

        def rs_copy(g, i):
            where = pl.ds(pl.multiple_of(sub_index(*SUBS[i]) * piece, 8), piece)
            return copy_to(part.at[s, g, where], rs_recv.at[s, g, i], rs_ssem.at[s, g], rs_rsem.at[s, g], subs[i])

        def ag_copy(g, i):
            return copy_to(dist.at[s, g, mine], dist.at[s, g, mine], ag_ssem.at[s, g], ag_rsem.at[s, g], subs[i])

        def gram(g):
            a = jnp.concatenate([block(d) for d in GROUPS[g]], axis=0)
            norms = jnp.sum(a * a, axis=1, keepdims=True)
            part[s, g] = dot3(split(a), (jh[...], jl[...]), NT) + norms + norms_j
            for i in range(7):
                rs_copy(g, i).start()

        def add_up(g):
            wait_bytes(rs_recv.at[s, g], rs_rsem.at[s, g])
            total = part[s, g, mine]
            for i in range(7):
                total = total + rs_recv[s, g, i]
            dist[s, g, mine] = total
            for i in range(7):
                ag_copy(g, i).start()

        gram(0)
        for chunk in range(CHUNKS):
            ring.advance(2, chunk)
        gram(1)
        add_up(0)
        for chunk in range(CHUNKS):
            ring.advance(3, chunk)
        if s == 0:
            for chunk in range(2):
                ring_g.advance(0, chunk)
        gram(2)
        add_up(1)
        for chunk in range(CHUNKS):
            ring.advance(4, chunk)
        gram(3)

        first = jnp.zeros((8, cols), F32)
        second = jnp.zeros((8, cols), F32)
        for d in range(8):
            b = block(d).reshape(rows // 8, 8, cols)
            first = first + jnp.sum(b, axis=0)
            second = second + jnp.sum(b * b, axis=0)
        sums[s, 0], sums[s, 1] = first, second

        def sums_copy(i):
            return copy_to(
                sums.at[s], sums_recv.at[s, i], s_ssem.at[s, 0], s_rsem.at[s, 0], (sibling, other, cross)[i]
            )

        def scal_copy(i):
            return copy_to(scal.at[s], scal_recv.at[s, i], s_ssem.at[s, 1], s_rsem.at[s, 1], subs[i])

        for i in range(3):
            sums_copy(i).start()
        if s == 0:
            for chunk in range(2):
                ring_g.advance(1, chunk)
        add_up(2)
        wait_bytes(sums_recv.at[s], s_rsem.at[s, 0])
        both = sums[s] + sums_recv[s, 0] + sums_recv[s, 1] + sums_recv[s, 2]
        first = jnp.sum(both[0], axis=0, keepdims=True)
        scal[s, 0] = jnp.broadcast_to(first * first, (8, cols))
        scal[s, 1] = both[1]
        for i in range(7):
            scal_copy(i).start()
        if s == 0:
            for chunk in range(2):
                ring_g.advance(2, chunk)
        add_up(3)
        if s == 0:
            for chunk in range(2):
                ring_g.advance(3, chunk)
            for chunk in range(2, 4):
                ring_g.advance(0, chunk)
        wait_bytes(scal_recv.at[s], s_rsem.at[s, 1])
        both = scal[s]
        for i in range(7):
            both = both + scal_recv[s, i]
        first_sq = jnp.sum(both[0, 0:1], axis=1, keepdims=True)
        second_all = jnp.sum(jnp.sum(both[1], axis=0, keepdims=True), axis=1, keepdims=True)
        width = (2.0 * count * second_all - 2.0 * first_sq) / (count * (count - 1.0)) / math.log(count + 1.0)

        def weights(g):
            wait_bytes(dist.at[s, g, pl.ds(0, 7 * piece)], ag_rsem.at[s, g])
            k = jnp.exp(-dist[s, g] / width)
            where = pl.ds(g * 2 * rows, 2 * rows)
            kh[where], kl[where] = split(k)

        def h_copy(part_of):
            return copy_to(
                half_send.at[s, part_of], half_recv.at[s, part_of], p_ssem.at[s, part_of, 2],
                p_rsem.at[s, part_of, 2], other,
            )

        def target(part_of):
            width_of = cols // 2
            lanes = pl.ds(part_of * width_of, width_of)
            for g in range(4):
                for e, d in enumerate(GROUPS[g]):
                    where = pl.ds((2 * g + e) * rows, rows)
                    th[where, lanes], tl[where, lanes] = split(make_target(d, lanes, width))

        def pulled(part_of):
            width_of = cols // 2
            lanes = pl.ds(part_of * width_of, width_of)
            result = dot3((kh[...], kl[...]), (th[:, lanes], tl[:, lanes]), TN)
            pull_s[part_of, :, :, 0:width_of] = result.reshape(4, rows, width_of)
            for side in range(2):
                p_copy(part_of, side).start()

        def across(part_of):
            p_copy(part_of, 1).wait_recv()
            half_send[s, part_of] = pull_s[part_of, 2] + sib_recv[s, part_of, 1]
            h_copy(part_of).start()

        def finish(part_of):
            p_copy(part_of, 0).wait_recv()
            h_copy(part_of).wait_recv()
            return pull_s[part_of, 0] + sib_recv[s, part_of, 0] + half_recv[s, part_of]

        pull_s = pull.at[s]

        def p_copy(part_of, side):
            return copy_to(
                pull_s.at[part_of, 1 + 2 * side], sib_recv.at[s, part_of, side], p_ssem.at[s, part_of, side],
                p_rsem.at[s, part_of, side], sibling,
            )

        weights(0)
        if s == 0:
            for chunk in range(2):
                ring_g.advance(4, chunk)
            for chunk in range(2, 4):
                ring_g.advance(1, chunk)
        weights(1)
        target(0)
        if s == 0:
            for chunk in range(2, 4):
                ring_g.advance(2, chunk)
        weights(2)
        if s == 0:
            for chunk in range(2, 4):
                ring_g.advance(3, chunk)
        weights(3)
        ones = jnp.ones((8 * rows, 128), BF16)
        dot = functools.partial(lax.dot_general, dimension_numbers=TN, preferred_element_type=F32)
        pull_s[0, :, :, cols // 2 :] = (dot(kl[...], ones) + dot(kh[...], ones)).reshape(4, rows, 128)
        pull_s[1, :, :, cols // 2 :] = jnp.zeros((4, rows, 128), F32)
        pulled(0)
        if s == 0:
            for chunk in range(2, 4):
                ring_g.advance(4, chunk)
        target(1)
        across(0)
        pulled(1)
        across(1)
        whole = finish(0)
        total = whole[:, cols // 2 : cols // 2 + 1]
        out[:, 0 : cols // 2] = 2.0 * own[:, 0 : cols // 2] + whole[:, 0 : cols // 2] / total
        whole = finish(1)
        out[:, cols // 2 :] = 2.0 * own[:, cols // 2 :] + whole[:, 0 : cols // 2] / total

        def drain():
            ring.drain()
            for k in range(1, 4):
                for chunk in range(2):
                    xj_copy(k, chunk).wait_send()
            for g in range(4):
                wait_bytes(part.at[s, g, pl.ds(0, 7 * piece)], rs_ssem.at[s, g])
                wait_bytes(part.at[s, g, pl.ds(0, 7 * piece)], ag_ssem.at[s, g])
            wait_bytes(sums_recv.at[s], s_ssem.at[s, 0])
            wait_bytes(scal_recv.at[s], s_ssem.at[s, 1])
            for part_of in range(2):
                for side in range(2):
                    p_copy(part_of, side).wait_send()
                h_copy(part_of).wait_send()

        return drain

    def target0(d, lanes, width):
        x = x_ref[:, lanes] if d == 0 else held0[d, :, lanes]
        g = g_ref[:, lanes] if d == 0 else heldg[d, :, lanes]
        return 0.5 * width * g - x

    def target1(d, lanes, width):
        x0 = x_ref[:, lanes] if d == 0 else held0[d, :, lanes]
        g = g_ref[:, lanes] if d == 0 else heldg[d, :, lanes]
        x = x1_ref[:, lanes] if d == 0 else held1[d, :, lanes]
        return 0.5 * width * (g - c_ref[0:1, lanes] * (x - x0)) - x

    drains = [stein(0, x_ref, held0, target0, x1_ref)]
    drains.append(stein(1, x1_ref, held1, target1, o_ref))
    for drain in drains:
        drain()
    ring_g.drain()


def shards(particles, gradient, curvature):
    rows, cols = particles.shape
    lanes_j = 4 * rows
    piece = 2 * rows // 8
    wide = cols // 2 + 128
    vmem = pl.BlockSpec(memory_space=pltpu.VMEM)
    dma = pltpu.SemaphoreType.DMA
    return pl.pallas_call(
        kernel,
        name="stein",
        out_shape=jax.ShapeDtypeStruct((rows, cols), F32),
        in_specs=[vmem] * 3,
        out_specs=vmem,
        scratch_shapes=[
            pltpu.VMEM((rows, cols), F32),
            pltpu.VMEM((8, rows, cols), F32),
            pltpu.VMEM((8, rows, cols), F32),
            pltpu.VMEM((8, rows, cols), F32),
            pltpu.VMEM((2, 4, rows, cols), F32),
            pltpu.VMEM((lanes_j, cols), BF16),
            pltpu.VMEM((lanes_j, cols), BF16),
            pltpu.VMEM((2, 4, 2 * rows, lanes_j), F32),
            pltpu.VMEM((2, 4, 2 * rows, lanes_j), F32),
            pltpu.VMEM((2, 4, 7, piece, lanes_j), F32),
            pltpu.VMEM((8 * rows, lanes_j), BF16),
            pltpu.VMEM((8 * rows, lanes_j), BF16),
            pltpu.VMEM((8 * rows, cols), BF16),
            pltpu.VMEM((8 * rows, cols), BF16),
            pltpu.VMEM((2, 2, 8, cols), F32),
            pltpu.VMEM((2, 3, 2, 8, cols), F32),
            pltpu.VMEM((2, 2, 8, cols), F32),
            pltpu.VMEM((2, 7, 2, 8, cols), F32),
            pltpu.VMEM((2, 2, 4, rows, wide), F32),
            pltpu.VMEM((2, 2, 2, rows, wide), F32),
            pltpu.VMEM((2, 2, rows, wide), F32),
            pltpu.VMEM((2, 2, rows, wide), F32),
            dma((3, 2, 4)),
            dma((3, 2, 4, CHUNKS)),
            dma((2, 4, 2)),
            dma((2, 4, 2)),
            dma((2, 4)),
            dma((2, 4)),
            dma((2, 4)),
            dma((2, 4)),
            dma((2, 2)),
            dma((2, 2)),
            dma((2, 2, 3)),
            dma((2, 2, 3)),
        ],
        compiler_params=pltpu.CompilerParams(
            collective_id=0, has_side_effects=True, vmem_limit_bytes=52 * 2**20
        ),
    )(particles, gradient, curvature.reshape(1, cols))


def solution(mesh):
    in_specs = (P("dom", "sub"), P("dom", "sub"), P("sub"))
    out_specs = P("dom", "sub")
    return jax.shard_map(shards, mesh=mesh, in_specs=in_specs, out_specs=out_specs, check_vma=False)
```

```python
import functools
import math

import jax
import jax.numpy as jnp
from jax import lax
from jax.experimental import pallas as pl
from jax.experimental.pallas import tpu as pltpu
from jax.sharding import PartitionSpec as P

F32, BF16 = jnp.float32, jnp.bfloat16
MESH = pl.DeviceIdType.MESH
NT = (((1,), (1,)), ((), ()))
NN = (((1,), (0,)), ((), ()))

GROUPS = ((1, 7), (2, 6), (3, 5), (0, 4))
SUBS = tuple((dx, dy) for dx in range(2) for dy in range(4))[1:]
CHUNKS = 4


def split(a):
    high = a.astype(BF16)
    return high, (a - high.astype(F32)).astype(BF16)


def dot3(a, b, dims):
    (ah, al), (bh, bl) = a, b
    dot = functools.partial(lax.dot_general, dimension_numbers=dims, preferred_element_type=F32)
    return dot(al, bh) + dot(ah, bl) + dot(ah, bh)


def copy_to(src, dst, send, recv, device):
    return pltpu.make_async_remote_copy(
        src_ref=src, dst_ref=dst, send_sem=send, recv_sem=recv, device_id=device, device_id_type=MESH
    )


def wait_bytes(ref, sem):
    pltpu.make_async_copy(ref, ref, sem).wait()


class Ring:
    def __init__(self, held, send, recv, sib_send, sib_recv, right, left, sibling):
        self.held, self.send, self.recv = held, send, recv
        self.sib_send, self.sib_recv = sib_send, sib_recv
        self.to, self.sibling = (right, left), sibling

    def piece(self, d, chunk):
        width = self.held.shape[3] // CHUNKS
        return self.held.at[0, d, :, pl.ds(chunk * width, width)]

    def has(self, way, step, chunk):
        return step < 3 or (step == 3 and (chunk % 2 == way))

    def copy(self, way, step, chunk):
        src = (-step) % 8 if way == 0 else step
        dst = (-step - 1) % 8 if way == 0 else step + 1
        return copy_to(
            self.piece(src, chunk), self.piece(dst, chunk), self.send.at[way, step], self.recv.at[way, step, chunk],
            self.to[way],
        )

    def advance(self, step, chunks=range(CHUNKS)):
        for chunk in chunks:
            for way in range(2):
                if step > 0 and self.has(way, step - 1, chunk):
                    self.copy(way, step - 1, chunk).wait_recv()
                if self.has(way, step, chunk):
                    self.copy(way, step, chunk).start()

    def sib_copy(self, d):
        return copy_to(self.held.at[0, d], self.held.at[1, d], self.sib_send.at[d], self.sib_recv.at[d], self.sibling)

    def hand(self, *blocks):
        for d in blocks:
            self.sib_copy(d).start()

    def wait_handed(self, *blocks):
        for d in blocks:
            self.sib_copy(d).wait_recv()

    def drain(self):
        block = self.held.at[0, 0]
        for way in range(2):
            for step in range(4):
                ref = block if step < 3 else block.at[pl.ds(0, block.shape[0] // 2)]
                wait_bytes(ref, self.send.at[way, step])
        for d in range(8):
            self.sib_copy(d).wait_send()


def kernel(
    x_ref, g_ref, c_ref, o_ref,
    hx, hg, cv, xo, jx, jh, jl, part, dist, rs_recv, th, tl, pull, p_recv, tot, t_send, t_recv,
    jsum, jsum_recv, zsum, zsum_recv, scal, scal_recv,
    ring_send, ring_recv, sib_send, sib_recv, xo_send, xo_recv, rs_ssem, rs_rsem, ag_ssem, ag_rsem,
    s_ssem, s_rsem, p_ssem, p_rsem, in_sem,
):
    rows, cols = o_ref.shape
    dom, sub = lax.axis_index("dom"), lax.axis_index("sub")
    core, z, half = dom % 2, (dom // 2) % 8, dom // 16
    y, pair = sub % 4, sub // 4
    count = 1.0 * rows * lax.axis_size("dom")
    piece = 2 * rows // 8
    mine = pl.ds(pl.multiple_of(sub * piece, 8), piece)
    own_rows = pl.ds(pl.multiple_of(core * rows, 16), rows)
    other_rows = pl.ds(pl.multiple_of((1 - core) * rows, 16), rows)
    adds_other = (pair + core) % 2

    def at(dh, dz, dc):
        return (((half + dh) % 2 * 8 + (z + dz) % 8) * 2 + (core + dc) % 2, sub)

    def sub_index(dx, dy):
        return (pair + dx) % 2 * 4 + (y + dy) % 4

    zs = [at(0, dz, 0) for dz in range(1, 8)]
    right, left, sibling, other = zs[0], zs[6], at(0, 0, 1), at(1, 0, 0)
    sub_at = [sub_index(dx, dy) for dx, dy in SUBS]
    subs = [(dom, i) for i in sub_at]

    moves = [
        pltpu.make_async_copy(src, dst, in_sem.at[i])
        for i, (src, dst) in enumerate(((x_ref, hx.at[0, 0, 0]), (g_ref, hg.at[0, 0]), (c_ref, cv)))
    ]
    for move in moves:
        move.start()
    barrier = pltpu.get_barrier_semaphore()
    partners = zs + [sibling, other] + subs
    for partner in partners:
        pl.semaphore_signal(barrier, inc=1, device_id=partner, device_id_type=MESH)
    for move in moves:
        move.wait()
    pl.semaphore_wait(barrier, len(partners))

    def ring_of(i, held):
        return Ring(
            held, ring_send.at[i], ring_recv.at[i], sib_send.at[i], sib_recv.at[i], right, left, sibling
        )

    rings = [ring_of(0, hx.at[0]), ring_of(1, hx.at[1])]
    ring_g = ring_of(2, hg)

    def lanes_of(hf):
        return pl.ds(hf * (cols // 2), cols // 2)

    def xo_copy(s, hf):
        return copy_to(
            hx.at[s, 0, 0, :, lanes_of(hf)], xo.at[s, :, lanes_of(hf)], xo_send.at[s, hf], xo_recv.at[s, hf], other
        )

    def begin(s, hf):
        xo_copy(s, hf).start()
        rings[s].advance(0, (2 * hf, 2 * hf + 1))

    def stein(s):
        ring = rings[s]

        def rs_copy(g, i):
            where = pl.ds(pl.multiple_of(sub_at[i] * piece, 8), piece)
            return copy_to(part.at[s, g, where], rs_recv.at[s, g, i], rs_ssem.at[s, g], rs_rsem.at[s, g], subs[i])

        def ag_copy(g, i):
            return copy_to(
                dist.at[s, g, mine], dist.at[s, g, mine], ag_ssem.at[s, g], ag_rsem.at[s, g, SUBS[i][0]], subs[i]
            )

        def members(g):
            return [(d, e) for d in GROUPS[g] for e in range(2)]

        def gram(g):
            a = jnp.concatenate([hx[s, e, d] for d, e in members(g)], axis=0)
            norms = jnp.sum(a * a, axis=1, keepdims=True)
            norms = jnp.broadcast_to(norms, (a.shape[0], 128)).T[0:1]
            part[s, g] = dot3((jh[...], jl[...]), split(a), NT) + norms_j + norms
            for i in range(7):
                rs_copy(g, i).start()

        def add_up(g):
            wait_bytes(rs_recv.at[s, g], rs_rsem.at[s, g])
            total = part[s, g, mine]
            for i in range(7):
                total = total + rs_recv[s, g, i]
            dist[s, g, mine] = total
            for i in range(7):
                ag_copy(g, i).start()

        def add_up_if(kind, *groups):
            @pl.when(adds_other == kind)
            def _():
                for g in groups:
                    add_up(g)

        def wait_rows(g, kind):
            @pl.when(adds_other == kind)
            def _():
                wait_bytes(dist.at[s, g, pl.ds(0, 3 * piece)], ag_rsem.at[s, g, 0])

            @pl.when(adds_other != kind)
            def _():
                wait_bytes(dist.at[s, g, pl.ds(0, 4 * piece)], ag_rsem.at[s, g, 1])

        def jsum_copy():
            return copy_to(jsum.at[s], jsum_recv.at[s], s_ssem.at[s, 0], s_rsem.at[s, 0], sibling)

        def zsum_copy(i):
            return copy_to(zsum.at[s], zsum_recv.at[s, i], s_ssem.at[s, 1], s_rsem.at[s, 1], zs[i])

        def scal_copy(i):
            return copy_to(scal.at[s], scal_recv.at[s, i], s_ssem.at[s, 2], s_rsem.at[s, 2], subs[i])

        ring.advance(1)
        ring.hand(1, 7)

        for hf in range(2):
            xo_copy(s, hf).wait_recv()
        jx[own_rows] = hx[s, 0, 0]
        jx[other_rows] = xo[s]
        js = jx[...]
        jh[...], jl[...] = split(-2.0 * js)
        squares = js * js
        norms_j = jnp.sum(squares, axis=1, keepdims=True)
        sums = [jnp.sum(a, axis=0, keepdims=True) for a in (js, squares)]
        jsum[s] = jnp.concatenate([a[:, k * 128 : k * 128 + 128] for a in sums for k in range(4)], axis=0)
        jsum_copy().start()

        ring.advance(2, (0, 1))
        ring.wait_handed(1, 7)
        gram(0)
        jsum_copy().wait_recv()
        zsum[s] = jsum[s] + jsum_recv[s]
        for i in range(7):
            zsum_copy(i).start()
        ring.advance(2, (2, 3))
        ring.hand(2, 6)
        ring.advance(3, (0,))
        ring.wait_handed(2, 6)
        gram(1)
        ring.advance(3, (1,))
        add_up_if(1, 0)
        ring.advance(3, (2, 3))
        ring.hand(3, 5)
        if s == 0:
            ring_g.advance(0)
            ring_g.hand(0)
        ring.wait_handed(3, 5)
        gram(2)
        ring.advance(4)
        ring.hand(4)
        add_up_if(1, 1)
        wait_bytes(zsum_recv.at[s], s_rsem.at[s, 1])
        both = zsum[s]
        for i in range(7):
            both = both + zsum_recv[s, i]
        scal[s, 0:4] = both[0:4] * both[0:4]
        scal[s, 4:8] = both[4:8]
        for i in range(7):
            scal_copy(i).start()
        ring.wait_handed(0, 4)
        gram(3)
        if s == 0:
            ring_g.advance(1)
            ring_g.hand(1, 7)
        add_up_if(1, 2)
        if s == 0:
            ring_g.advance(2)
            ring_g.hand(2, 6)
        add_up_if(1, 3)
        add_up_if(0, 0, 1, 2, 3)
        wait_bytes(scal_recv.at[s], s_rsem.at[s, 2])
        both = scal[s]
        for i in range(7):
            both = both + scal_recv[s, i]
        both = jnp.sum(both, axis=1, keepdims=True)
        first_sq = jnp.sum(both[0:4], axis=0, keepdims=True)
        second_all = jnp.sum(both[4:8], axis=0, keepdims=True)
        width = (2.0 * count * second_all - 2.0 * first_sq) / (count * (count - 1.0)) / math.log(count + 1.0)

        whole = pl.ds(0, cols)

        def target(d, e, lanes):
            x, g = hx[s, e, d, :, lanes], hg[e, d, :, lanes]
            if s == 1:
                g = g - cv[0:1, lanes] * (x - hx[0, e, d, :, lanes])
            return 0.5 * width * g - x

        def targets(g):
            t = jnp.concatenate([target(d, e, whole) for d, e in members(g)], axis=0)
            th[g], tl[g] = split(t)

        def weights(g, kind):
            wait_rows(g, kind)
            k = jnp.exp(-dist[s, g, other_rows if kind else own_rows] / width)
            total = jnp.broadcast_to(jnp.sum(k, axis=1, keepdims=True), (rows, 128))
            tot[kind, 128 - rows :] = total if g == 0 else tot[kind, 128 - rows :] + total
            return split(k)

        def pulled(g, kind, k, lanes):
            where = other_rows if kind else own_rows
            result = dot3(k, (th[g, :, lanes], tl[g, :, lanes]), NN)
            pull[s, where, lanes] = result if g == 0 else pull[s, where, lanes] + result

        def p_copy(hf):
            return copy_to(
                pull.at[s, other_rows, lanes_of(hf)], p_recv.at[s, :, lanes_of(hf)], p_ssem.at[s, hf],
                p_rsem.at[s, hf], other,
            )

        def t_copy():
            return copy_to(t_send.at[s], t_recv.at[s], p_ssem.at[s, 2], p_rsem.at[s, 2], other)

        tot[1, 0 : 128 - rows] = jnp.zeros((128 - rows, 128), F32)
        for g in range(4):
            if s == 0:
                ring_g.wait_handed(*GROUPS[g])
            if s == 0 and g == 0:
                ring_g.advance(3)
                ring_g.hand(3, 5)
            targets(g)
            k = weights(g, 1)
            if g < 3:
                pulled(g, 1, k, whole)
            if s == 0 and g == 1:
                ring_g.advance(4)
                ring_g.hand(4)
        t_send[s] = tot[1].T[0:8]
        t_copy().start()
        for hf in range(2):
            pulled(3, 1, k, lanes_of(hf))
            p_copy(hf).start()
        for g in range(4):
            pulled(g, 0, weights(g, 0), whole)
        t_copy().wait_recv()
        theirs = jnp.broadcast_to(t_recv[s, 0:1], (128, 128)).T[128 - rows :, 0:1]
        total = tot[0, 128 - rows :, 0:1] + theirs
        for hf in range(2):
            lanes = lanes_of(hf)
            p_copy(hf).wait_recv()
            moved = 2.0 * hx[s, 0, 0, :, lanes] + (pull[s, own_rows, lanes] + p_recv[s, :, lanes]) / total
            if s == 0:
                hx[1, 0, 0, :, lanes] = moved
                begin(1, hf)
            else:
                o_ref[:, lanes] = moved
        if s == 0:
            rings[1].hand(0)

        def drain():
            ring.drain()
            for hf in range(2):
                xo_copy(s, hf).wait_send()
                p_copy(hf).wait_send()
            t_copy().wait_send()
            for g in range(4):
                wait_bytes(part.at[s, g, pl.ds(0, 7 * piece)], rs_ssem.at[s, g])
                wait_bytes(part.at[s, g, pl.ds(0, 7 * piece)], ag_ssem.at[s, g])
            jsum_copy().wait_send()
            wait_bytes(zsum_recv.at[s], s_ssem.at[s, 1])
            wait_bytes(scal_recv.at[s], s_ssem.at[s, 2])

        return drain

    for hf in range(2):
        begin(0, hf)
    rings[0].hand(0)
    drains = [stein(0), stein(1), ring_g.drain]
    for drain in drains:
        drain()


def shards(particles, gradient, curvature):
    rows, cols = particles.shape
    near, far = 2 * rows, 4 * rows
    piece = near // 8
    vmem = pl.BlockSpec(memory_space=pltpu.VMEM)
    dma = pltpu.SemaphoreType.DMA
    return pl.pallas_call(
        kernel,
        name="stein",
        out_shape=jax.ShapeDtypeStruct((rows, cols), F32),
        in_specs=[pl.BlockSpec(memory_space=pltpu.HBM)] * 3,
        out_specs=vmem,
        scratch_shapes=[
            pltpu.VMEM((2, 2, 8, rows, cols), F32),
            pltpu.VMEM((2, 8, rows, cols), F32),
            pltpu.VMEM((1, cols), F32),
            pltpu.VMEM((2, rows, cols), F32),
            pltpu.VMEM((near, cols), F32),
            pltpu.VMEM((near, cols), BF16),
            pltpu.VMEM((near, cols), BF16),
            pltpu.VMEM((2, 4, near, far), F32),
            pltpu.VMEM((2, 4, near, far), F32),
            pltpu.VMEM((2, 4, 7, piece, far), F32),
            pltpu.VMEM((4, far, cols), BF16),
            pltpu.VMEM((4, far, cols), BF16),
            pltpu.VMEM((2, near, cols), F32),
            pltpu.VMEM((2, rows, cols), F32),
            pltpu.VMEM((2, 128, 128), F32),
            pltpu.VMEM((2, 8, 128), F32),
            pltpu.VMEM((2, 8, 128), F32),
            pltpu.VMEM((2, 8, 128), F32),
            pltpu.VMEM((2, 8, 128), F32),
            pltpu.VMEM((2, 8, 128), F32),
            pltpu.VMEM((2, 7, 8, 128), F32),
            pltpu.VMEM((2, 8, 128), F32),
            pltpu.VMEM((2, 7, 8, 128), F32),
            dma((3, 2, 4)),
            dma((3, 2, 4, CHUNKS)),
            dma((3, 8)),
            dma((3, 8)),
            dma((2, 2)),
            dma((2, 2)),
            dma((2, 4)),
            dma((2, 4)),
            dma((2, 4)),
            dma((2, 4, 2)),
            dma((2, 3)),
            dma((2, 3)),
            dma((2, 3)),
            dma((2, 3)),
            dma((3,)),
        ],
        compiler_params=pltpu.CompilerParams(
            collective_id=0, has_side_effects=True, vmem_limit_bytes=63 * 2**20 + 2**19
        ),
    )(particles, gradient, curvature.reshape(1, cols))


def solution(mesh):
    in_specs = (P("dom", "sub"), P("dom", "sub"), P("sub"))
    out_specs = P("dom", "sub")
    return jax.shard_map(shards, mesh=mesh, in_specs=in_specs, out_specs=out_specs, check_vma=False)
```

```python
import functools
import math

import jax
import jax.numpy as jnp
from jax import lax
from jax.experimental import pallas as pl
from jax.experimental.pallas import tpu as pltpu
from jax.sharding import PartitionSpec as P

F32, BF16 = jnp.float32, jnp.bfloat16
MESH = pl.DeviceIdType.MESH
NT = (((1,), (1,)), ((), ()))
NN = (((1,), (0,)), ((), ()))

GROUPS = ((1, 7), (2, 6), (3, 5), (0, 4))
SUBS = tuple((dx, dy) for dx in range(2) for dy in range(4))[1:]
CHUNKS = 4


def split(a):
    high = a.astype(BF16)
    return high, (a - high.astype(F32)).astype(BF16)


def dot3(a, b, dims):
    (ah, al), (bh, bl) = a, b
    dot = functools.partial(lax.dot_general, dimension_numbers=dims, preferred_element_type=F32)
    return dot(al, bh) + dot(ah, bl) + dot(ah, bh)


def copy_to(src, dst, send, recv, device):
    return pltpu.make_async_remote_copy(
        src_ref=src, dst_ref=dst, send_sem=send, recv_sem=recv, device_id=device, device_id_type=MESH
    )


def wait_bytes(ref, sem):
    pltpu.make_async_copy(ref, ref, sem).wait()


class Ring:
    def __init__(self, held, send, recv, sib_send, sib_recv, right, left, sibling):
        self.held, self.send, self.recv = held, send, recv
        self.sib_send, self.sib_recv = sib_send, sib_recv
        self.to, self.sibling = (right, left), sibling

    def piece(self, d, chunk):
        width = self.held.shape[3] // CHUNKS
        return self.held.at[0, d, :, pl.ds(chunk * width, width)]

    def has(self, way, step, chunk):
        return step < 3 or (step == 3 and (chunk % 2 == way))

    def copy(self, way, step, chunk):
        src = (-step) % 8 if way == 0 else step
        dst = (-step - 1) % 8 if way == 0 else step + 1
        return copy_to(
            self.piece(src, chunk), self.piece(dst, chunk), self.send.at[way, step], self.recv.at[way, step, chunk],
            self.to[way],
        )

    def advance(self, step, chunks=range(CHUNKS)):
        for chunk in chunks:
            for way in range(2):
                if step > 0 and self.has(way, step - 1, chunk):
                    self.copy(way, step - 1, chunk).wait_recv()
                if self.has(way, step, chunk):
                    self.copy(way, step, chunk).start()

    def sib_copy(self, d):
        return copy_to(self.held.at[0, d], self.held.at[1, d], self.sib_send.at[d], self.sib_recv.at[d], self.sibling)

    def hand(self, *blocks):
        for d in blocks:
            self.sib_copy(d).start()

    def wait_handed(self, *blocks):
        for d in blocks:
            self.sib_copy(d).wait_recv()

    def drain(self):
        block = self.held.at[0, 0]
        for way in range(2):
            for step in range(4):
                ref = block if step < 3 else block.at[pl.ds(0, block.shape[0] // 2)]
                wait_bytes(ref, self.send.at[way, step])
        for d in range(8):
            self.sib_copy(d).wait_send()


def kernel(
    x_ref, g_ref, c_ref, o_ref,
    hx, hg, cv, xo, jx, jh, jl, part, dist, rs_recv, th, tl, pull, p_recv, tot, t_send, t_recv,
    sums, half_sum, half_recv, scal, scal_recv,
    ring_send, ring_recv, sib_send, sib_recv, xo_send, xo_recv, rs_ssem, rs_rsem, ag_ssem, ag_rsem,
    near_rsem, fwd_ssem, s_ssem, s_rsem, p_ssem, p_rsem, in_sem,
):
    rows, cols = o_ref.shape
    dom, sub = lax.axis_index("dom"), lax.axis_index("sub")
    core, z, half = dom % 2, (dom // 2) % 8, dom // 16
    y, pair = sub % 4, sub // 4
    count = 1.0 * rows * lax.axis_size("dom")
    piece = 2 * rows // 8
    mine = pl.ds(pl.multiple_of(sub * piece, 8), piece)
    own_rows = pl.ds(pl.multiple_of(core * rows, 16), rows)
    other_rows = pl.ds(pl.multiple_of((1 - core) * rows, 16), rows)
    adds_other = (pair + core) % 2

    def at(dh, dz, dc):
        return (((half + dh) % 2 * 8 + (z + dz) % 8) * 2 + (core + dc) % 2, sub)

    def sub_index(dx, dy):
        return (pair + dx) % 2 * 4 + (y + dy) % 4

    right, left, sibling, other = at(0, 1, 0), at(0, 7, 0), at(0, 0, 1), at(1, 0, 0)
    sub_at = [sub_index(dx, dy) for dx, dy in SUBS]
    subs = [(dom, i) for i in sub_at]

    moves = [
        pltpu.make_async_copy(src, dst, in_sem.at[i])
        for i, (src, dst) in enumerate(((x_ref, hx.at[0, 0, 0]), (g_ref, hg.at[0, 0]), (c_ref, cv)))
    ]
    for move in moves:
        move.start()
    barrier = pltpu.get_barrier_semaphore()
    partners = [right, left, sibling, other] + subs
    for partner in partners:
        pl.semaphore_signal(barrier, inc=1, device_id=partner, device_id_type=MESH)
    for move in moves:
        move.wait()
    pl.semaphore_wait(barrier, len(partners))

    def ring_of(i, held):
        return Ring(
            held, ring_send.at[i], ring_recv.at[i], sib_send.at[i], sib_recv.at[i], right, left, sibling
        )

    rings = [ring_of(0, hx.at[0]), ring_of(1, hx.at[1])]
    ring_g = ring_of(2, hg)

    def lanes_of(hf):
        return pl.ds(hf * (cols // 2), cols // 2)

    def xo_copy(s, hf):
        return copy_to(
            hx.at[s, 0, 0, :, lanes_of(hf)], xo.at[s, :, lanes_of(hf)], xo_send.at[s, hf], xo_recv.at[s, hf], other
        )

    def begin(s, hf):
        xo_copy(s, hf).start()
        rings[s].advance(0, (2 * hf, 2 * hf + 1))

    def stein(s):
        ring = rings[s]

        def rs_copy(g, i):
            where = pl.ds(pl.multiple_of(sub_at[i] * piece, 8), piece)
            return copy_to(part.at[s, g, where], rs_recv.at[s, g, i], rs_ssem.at[s, g], rs_rsem.at[s, g], subs[i])

        def ag_copy(g, i):
            return copy_to(
                dist.at[s, g, mine], dist.at[s, g, mine], ag_ssem.at[s, g], ag_rsem.at[s, g, SUBS[i][0]], subs[i]
            )

        def members(g):
            return [(d, e) for d in GROUPS[g] for e in range(2)]

        def gram(g):
            a = jnp.concatenate([hx[s, e, d] for d, e in members(g)], axis=0)
            squares = a * a
            for k, b in enumerate((a, squares)):
                folded = jnp.sum(b.reshape(b.shape[0] // 8, 8, cols), axis=0)
                sums[k] = folded if g == 0 else sums[k] + folded
            norms = jnp.sum(squares, axis=1, keepdims=True)
            norms = jnp.broadcast_to(norms, (a.shape[0], 128)).T[0:1]
            part[s, g] = dot3((jh[...], jl[...]), split(a), NT) + norms_j + norms
            for i in range(7):
                rs_copy(g, i).start()

        def near_copy(g):
            here = dist.at[s, g, mine]
            return copy_to(here, here, ag_ssem.at[s, g], near_rsem.at[s, g], subs[3])

        def forward(g):
            @pl.when(adds_other == 1)
            def _():
                here = dist.at[s, g, pl.ds(pl.multiple_of(((pair + 1) % 2 * 4 + y) * piece, 8), piece)]
                wait_bytes(here, near_rsem.at[s, g])
                for i in range(3):
                    copy_to(here, here, fwd_ssem.at[s, g], ag_rsem.at[s, g, 1], subs[i]).start()

        def add_up(g):
            wait_bytes(rs_recv.at[s, g], rs_rsem.at[s, g])
            total = part[s, g, mine]
            for i in range(7):
                total = total + rs_recv[s, g, i]
            dist[s, g, mine] = total
            for i in range(3):
                ag_copy(g, i).start()

            @pl.when(adds_other == 1)
            def _():
                for i in range(3, 7):
                    ag_copy(g, i).start()

            @pl.when(adds_other == 0)
            def _():
                near_copy(g).start()

        def add_up_if(kind, *groups):
            @pl.when(adds_other == kind)
            def _():
                for g in groups:
                    add_up(g)

        def wait_rows(g, kind):
            if kind == 0:
                wait_bytes(dist.at[s, g, pl.ds(0, 3 * piece)], ag_rsem.at[s, g, adds_other])
                return

            @pl.when(adds_other == kind)
            def _():
                wait_bytes(dist.at[s, g, pl.ds(0, 3 * piece)], ag_rsem.at[s, g, 0])

            @pl.when(adds_other != kind)
            def _():
                wait_bytes(dist.at[s, g, pl.ds(0, 4 * piece)], ag_rsem.at[s, g, 1])

        def half_copy():
            return copy_to(half_sum.at[s], half_recv.at[s], s_ssem.at[s, 0], s_rsem.at[s, 0], other)

        def scal_copy(i):
            return copy_to(scal.at[s], scal_recv.at[s, i], s_ssem.at[s, 1], s_rsem.at[s, 1], subs[i])

        ring.advance(1)
        ring.hand(1, 7)

        for hf in range(2):
            xo_copy(s, hf).wait_recv()
        jx[own_rows] = hx[s, 0, 0]
        jx[other_rows] = xo[s]
        js = jx[...]
        jh[...], jl[...] = split(-2.0 * js)
        norms_j = jnp.sum(js * js, axis=1, keepdims=True)

        ring.advance(2, (0, 1))
        ring.wait_handed(1, 7)
        gram(0)
        ring.advance(2, (2, 3))
        ring.hand(2, 6)
        ring.advance(3, (0,))
        ring.wait_handed(2, 6)
        gram(1)
        ring.advance(3, (1,))
        add_up_if(1, 0)
        ring.advance(3, (2, 3))
        ring.hand(3, 5)
        if s == 0:
            ring_g.advance(0)
            ring_g.hand(0)
        ring.wait_handed(3, 5)
        gram(2)
        ring.advance(4)
        ring.hand(4)
        add_up_if(1, 1)
        ring.wait_handed(0, 4)
        gram(3)
        whole_sums = [jnp.sum(sums[k], axis=0, keepdims=True) for k in range(2)]
        half_sum[s] = jnp.concatenate([a[:, k * 128 : k * 128 + 128] for a in whole_sums for k in range(4)], axis=0)
        half_copy().start()
        if s == 0:
            ring_g.advance(1)
            ring_g.hand(1, 7)
        add_up_if(1, 2)
        half_copy().wait_recv()
        both = half_sum[s] + half_recv[s]
        scal[s, 0:4] = both[0:4] * both[0:4]
        scal[s, 4:8] = both[4:8]
        for i in range(7):
            scal_copy(i).start()
        if s == 0:
            ring_g.advance(2)
            ring_g.hand(2, 6)
        add_up_if(1, 3)
        add_up_if(0, 0, 1, 2, 3)
        wait_bytes(scal_recv.at[s], s_rsem.at[s, 1])
        both = scal[s]
        for i in range(7):
            both = both + scal_recv[s, i]
        both = jnp.sum(both, axis=1, keepdims=True)
        first_sq = jnp.sum(both[0:4], axis=0, keepdims=True)
        second_all = jnp.sum(both[4:8], axis=0, keepdims=True)
        width = (2.0 * count * second_all - 2.0 * first_sq) / (count * (count - 1.0)) / math.log(count + 1.0)

        whole = pl.ds(0, cols)

        def target(d, e, lanes):
            x, g = hx[s, e, d, :, lanes], hg[e, d, :, lanes]
            if s == 1:
                g = g - cv[0:1, lanes] * (x - hx[0, e, d, :, lanes])
            return 0.5 * width * g - x

        def targets(g):
            t = jnp.concatenate([target(d, e, whole) for d, e in members(g)], axis=0)
            th[g], tl[g] = split(t)

        def weights(g, kind):
            wait_rows(g, kind)
            k = jnp.exp(-dist[s, g, other_rows if kind else own_rows] / width)
            total = jnp.broadcast_to(jnp.sum(k, axis=1, keepdims=True), (rows, 128))
            tot[kind, 128 - rows :] = total if g == 0 else tot[kind, 128 - rows :] + total
            return split(k)

        def pulled(g, kind, k, lanes):
            where = other_rows if kind else own_rows
            result = dot3(k, (th[g, :, lanes], tl[g, :, lanes]), NN)
            pull[s, where, lanes] = result if g == 0 else pull[s, where, lanes] + result

        def p_copy(hf):
            return copy_to(
                pull.at[s, other_rows, lanes_of(hf)], p_recv.at[s, :, lanes_of(hf)], p_ssem.at[s, hf],
                p_rsem.at[s, hf], other,
            )

        def t_copy():
            return copy_to(t_send.at[s], t_recv.at[s], p_ssem.at[s, 2], p_rsem.at[s, 2], other)

        tot[1, 0 : 128 - rows] = jnp.zeros((128 - rows, 128), F32)
        for g in range(4):
            if s == 0:
                ring_g.wait_handed(*GROUPS[g])
            if s == 0 and g == 0:
                ring_g.advance(3)
                ring_g.hand(3, 5)
            if g == 3:
                forward(3)
            targets(g)
            k = weights(g, 1)
            if g < 3:
                pulled(g, 1, k, whole)
                forward(g)
            if s == 0 and g == 1:
                ring_g.advance(4)
                ring_g.hand(4)
        t_send[s] = tot[1].T[0:8]
        t_copy().start()
        for hf in range(2):
            pulled(3, 1, k, lanes_of(hf))
            p_copy(hf).start()
        for g in range(4):
            pulled(g, 0, weights(g, 0), whole)
        t_copy().wait_recv()
        theirs = jnp.broadcast_to(t_recv[s, 0:1], (128, 128)).T[128 - rows :, 0:1]
        total = tot[0, 128 - rows :, 0:1] + theirs
        for hf in range(2):
            lanes = lanes_of(hf)
            p_copy(hf).wait_recv()
            moved = 2.0 * hx[s, 0, 0, :, lanes] + (pull[s, own_rows, lanes] + p_recv[s, :, lanes]) / total
            if s == 0:
                hx[1, 0, 0, :, lanes] = moved
                begin(1, hf)
            else:
                o_ref[:, lanes] = moved
        if s == 0:
            rings[1].hand(0)

        def drain():
            ring.drain()
            for hf in range(2):
                xo_copy(s, hf).wait_send()
                p_copy(hf).wait_send()
            t_copy().wait_send()
            for g in range(4):
                wait_bytes(part.at[s, g, pl.ds(0, 7 * piece)], rs_ssem.at[s, g])

                @pl.when(adds_other == 1)
                def _():
                    wait_bytes(part.at[s, g, pl.ds(0, 7 * piece)], ag_ssem.at[s, g])
                    wait_bytes(part.at[s, g, pl.ds(0, 3 * piece)], fwd_ssem.at[s, g])

                @pl.when(adds_other == 0)
                def _():
                    wait_bytes(part.at[s, g, pl.ds(0, 4 * piece)], ag_ssem.at[s, g])
            half_copy().wait_send()
            wait_bytes(scal_recv.at[s], s_ssem.at[s, 1])

        return drain

    for hf in range(2):
        begin(0, hf)
    rings[0].hand(0)
    drains = [stein(0), stein(1), ring_g.drain]
    for drain in drains:
        drain()


def shards(particles, gradient, curvature):
    rows, cols = particles.shape
    near, far = 2 * rows, 4 * rows
    piece = near // 8
    vmem = pl.BlockSpec(memory_space=pltpu.VMEM)
    dma = pltpu.SemaphoreType.DMA
    return pl.pallas_call(
        kernel,
        name="stein",
        out_shape=jax.ShapeDtypeStruct((rows, cols), F32),
        in_specs=[pl.BlockSpec(memory_space=pltpu.HBM)] * 3,
        out_specs=vmem,
        scratch_shapes=[
            pltpu.VMEM((2, 2, 8, rows, cols), F32),
            pltpu.VMEM((2, 8, rows, cols), F32),
            pltpu.VMEM((1, cols), F32),
            pltpu.VMEM((2, rows, cols), F32),
            pltpu.VMEM((near, cols), F32),
            pltpu.VMEM((near, cols), BF16),
            pltpu.VMEM((near, cols), BF16),
            pltpu.VMEM((2, 4, near, far), F32),
            pltpu.VMEM((2, 4, near, far), F32),
            pltpu.VMEM((2, 4, 7, piece, far), F32),
            pltpu.VMEM((4, far, cols), BF16),
            pltpu.VMEM((4, far, cols), BF16),
            pltpu.VMEM((2, near, cols), F32),
            pltpu.VMEM((2, rows, cols), F32),
            pltpu.VMEM((2, 128, 128), F32),
            pltpu.VMEM((2, 8, 128), F32),
            pltpu.VMEM((2, 8, 128), F32),
            pltpu.VMEM((2, 8, cols), F32),
            pltpu.VMEM((2, 8, 128), F32),
            pltpu.VMEM((2, 8, 128), F32),
            pltpu.VMEM((2, 8, 128), F32),
            pltpu.VMEM((2, 7, 8, 128), F32),
            dma((3, 2, 4)),
            dma((3, 2, 4, CHUNKS)),
            dma((3, 8)),
            dma((3, 8)),
            dma((2, 2)),
            dma((2, 2)),
            dma((2, 4)),
            dma((2, 4)),
            dma((2, 4)),
            dma((2, 4, 2)),
            dma((2, 4)),
            dma((2, 4)),
            dma((2, 2)),
            dma((2, 2)),
            dma((2, 3)),
            dma((2, 3)),
            dma((3,)),
        ],
        compiler_params=pltpu.CompilerParams(
            collective_id=0, has_side_effects=True, vmem_limit_bytes=63 * 2**20 + 2**19
        ),
    )(particles, gradient, curvature.reshape(1, cols))


def solution(mesh):
    in_specs = (P("dom", "sub"), P("dom", "sub"), P("sub"))
    out_specs = P("dom", "sub")
    return jax.shard_map(shards, mesh=mesh, in_specs=in_specs, out_specs=out_specs, check_vma=False)
```

```python
import functools
import math

import jax
import jax.numpy as jnp
from jax import lax
from jax.experimental import pallas as pl
from jax.experimental.pallas import tpu as pltpu
from jax.sharding import PartitionSpec as P

F32, BF16 = jnp.float32, jnp.bfloat16
MESH = pl.DeviceIdType.MESH
NT = (((1,), (1,)), ((), ()))
NN = (((1,), (0,)), ((), ()))

GROUPS = ((1, 7), (2, 6), (3, 5), (0, 4))
SUBS = tuple((dx, dy) for dx in range(2) for dy in range(4))[1:]
CHUNKS = 4


def split(a):
    high = a.astype(BF16)
    return high, (a - high.astype(F32)).astype(BF16)


def dot3(a, b, dims):
    (ah, al), (bh, bl) = a, b
    dot = functools.partial(lax.dot_general, dimension_numbers=dims, preferred_element_type=F32)
    return dot(al, bh) + dot(ah, bl) + dot(ah, bh)


def copy_to(src, dst, send, recv, device):
    return pltpu.make_async_remote_copy(
        src_ref=src, dst_ref=dst, send_sem=send, recv_sem=recv, device_id=device, device_id_type=MESH
    )


def wait_bytes(ref, sem):
    pltpu.make_async_copy(ref, ref, sem).wait()


class Ring:
    def __init__(self, held, send, recv, sib_send, sib_recv, right, left, sibling):
        self.held, self.send, self.recv = held, send, recv
        self.sib_send, self.sib_recv = sib_send, sib_recv
        self.to, self.sibling = (right, left), sibling

    def piece(self, d, chunk):
        width = self.held.shape[3] // CHUNKS
        return self.held.at[0, d, :, pl.ds(chunk * width, width)]

    def has(self, way, step, chunk):
        return step < 3 or (step == 3 and (chunk % 2 == way))

    def copy(self, way, step, chunk):
        src = (-step) % 8 if way == 0 else step
        dst = (-step - 1) % 8 if way == 0 else step + 1
        return copy_to(
            self.piece(src, chunk), self.piece(dst, chunk), self.send.at[way, step], self.recv.at[way, step, chunk],
            self.to[way],
        )

    def advance(self, step, chunks=range(CHUNKS)):
        for chunk in chunks:
            for way in range(2):
                if step > 0 and self.has(way, step - 1, chunk):
                    self.copy(way, step - 1, chunk).wait_recv()
                if self.has(way, step, chunk):
                    self.copy(way, step, chunk).start()

    def sib_copy(self, d):
        return copy_to(self.held.at[0, d], self.held.at[1, d], self.sib_send.at[d], self.sib_recv.at[d], self.sibling)

    def hand(self, *blocks):
        for d in blocks:
            self.sib_copy(d).start()

    def finish(self):
        width = self.held.shape[3] // 2
        for hf in range(2):
            self.advance(4, (2 * hf, 2 * hf + 1))
            lanes = pl.ds(hf * width, width)
            copy_to(
                self.held.at[0, 4, :, lanes], self.held.at[1, 4, :, lanes], self.sib_send.at[4], self.sib_recv.at[4],
                self.sibling,
            ).start()

    def wait_handed(self, *blocks):
        for d in blocks:
            self.sib_copy(d).wait_recv()

    def drain(self):
        block = self.held.at[0, 0]
        for way in range(2):
            for step in range(4):
                ref = block if step < 3 else block.at[pl.ds(0, block.shape[0] // 2)]
                wait_bytes(ref, self.send.at[way, step])
        for d in range(8):
            self.sib_copy(d).wait_send()


def kernel(
    x_ref, g_ref, c_ref, o_ref,
    hx, hg, cv, xo, jx, jh, jl, part, dist, rs_recv, th, tl, pull, p_recv, tot, t_send, t_recv,
    sums, half_sum, half_recv, scal, scal_recv,
    ring_send, ring_recv, sib_send, sib_recv, xo_send, xo_recv, rs_ssem, rs_rsem, ag_ssem, ag_rsem,
    near_rsem, fwd_ssem, s_ssem, s_rsem, p_ssem, p_rsem, in_sem,
):
    rows, cols = o_ref.shape
    dom, sub = lax.axis_index("dom"), lax.axis_index("sub")
    core, z, half = dom % 2, (dom // 2) % 8, dom // 16
    y, pair = sub % 4, sub // 4
    count = 1.0 * rows * lax.axis_size("dom")
    piece = 2 * rows // 8
    mine = pl.ds(pl.multiple_of(sub * piece, 8), piece)
    own_rows = pl.ds(pl.multiple_of(core * rows, 16), rows)
    other_rows = pl.ds(pl.multiple_of((1 - core) * rows, 16), rows)
    adds_other = (pair + core) % 2

    def at(dh, dz, dc):
        return (((half + dh) % 2 * 8 + (z + dz) % 8) * 2 + (core + dc) % 2, sub)

    def sub_index(dx, dy):
        return (pair + dx) % 2 * 4 + (y + dy) % 4

    right, left, sibling, other = at(0, 1, 0), at(0, 7, 0), at(0, 0, 1), at(1, 0, 0)
    sub_at = [sub_index(dx, dy) for dx, dy in SUBS]
    subs = [(dom, i) for i in sub_at]

    moves = [
        pltpu.make_async_copy(src, dst, in_sem.at[i])
        for i, (src, dst) in enumerate(((x_ref, hx.at[0, 0, 0]), (g_ref, hg.at[0, 0]), (c_ref, cv)))
    ]
    for move in moves:
        move.start()
    barrier = pltpu.get_barrier_semaphore()
    partners = [right, left, sibling, other] + subs
    for partner in partners:
        pl.semaphore_signal(barrier, inc=1, device_id=partner, device_id_type=MESH)
    for move in moves:
        move.wait()
    pl.semaphore_wait(barrier, len(partners))

    def ring_of(i, held):
        return Ring(
            held, ring_send.at[i], ring_recv.at[i], sib_send.at[i], sib_recv.at[i], right, left, sibling
        )

    rings = [ring_of(0, hx.at[0]), ring_of(1, hx.at[1])]
    ring_g = ring_of(2, hg)

    def lanes_of(hf):
        return pl.ds(hf * (cols // 2), cols // 2)

    def xo_copy(s, hf):
        return copy_to(
            hx.at[s, 0, 0, :, lanes_of(hf)], xo.at[s, :, lanes_of(hf)], xo_send.at[s, hf], xo_recv.at[s, hf], other
        )

    def begin(s, hf):
        xo_copy(s, hf).start()
        rings[s].advance(0, (2 * hf, 2 * hf + 1))

    def stein(s):
        ring = rings[s]

        def rs_copy(g, i):
            where = pl.ds(pl.multiple_of(sub_at[i] * piece, 8), piece)
            return copy_to(part.at[s, g, where], rs_recv.at[s, g, i], rs_ssem.at[s, g], rs_rsem.at[s, g], subs[i])

        def ag_copy(g, i):
            return copy_to(
                dist.at[s, g, mine], dist.at[s, g, mine], ag_ssem.at[s, g], ag_rsem.at[s, g, SUBS[i][0]], subs[i]
            )

        def members(g):
            return [(d, e) for d in GROUPS[g] for e in range(2)]

        def gram(g):
            a = jnp.concatenate([hx[s, e, d] for d, e in members(g)], axis=0)
            squares = a * a
            for k, b in enumerate((a, squares)):
                folded = jnp.sum(b.reshape(b.shape[0] // 8, 8, cols), axis=0)
                sums[k] = folded if g == 0 else sums[k] + folded
            norms = jnp.sum(squares, axis=1, keepdims=True)
            norms = jnp.broadcast_to(norms, (a.shape[0], 128)).T[0:1]
            part[s, g] = dot3((jh[...], jl[...]), split(a), NT) + norms_j + norms

            @pl.when(adds_other == 1)
            def _():
                for i in range(7):
                    rs_copy(g, i).start()

            @pl.when(adds_other == 0)
            def _():
                for i in (3, 4, 5, 6, 0, 1, 2):
                    rs_copy(g, i).start()

        def near_copy(g):
            here = dist.at[s, g, mine]
            return copy_to(here, here, ag_ssem.at[s, g], near_rsem.at[s, g], subs[3])

        def forward(g):
            @pl.when(adds_other == 1)
            def _():
                here = dist.at[s, g, pl.ds(pl.multiple_of(((pair + 1) % 2 * 4 + y) * piece, 8), piece)]
                wait_bytes(here, near_rsem.at[s, g])
                for i in range(3):
                    copy_to(here, here, fwd_ssem.at[s, g], ag_rsem.at[s, g, 1], subs[i]).start()

        def add_up(g):
            wait_bytes(rs_recv.at[s, g], rs_rsem.at[s, g])
            total = part[s, g, mine]
            for i in range(7):
                total = total + rs_recv[s, g, i]
            dist[s, g, mine] = total
            for i in range(3):
                ag_copy(g, i).start()

            @pl.when(adds_other == 1)
            def _():
                for i in range(3, 7):
                    ag_copy(g, i).start()

            @pl.when(adds_other == 0)
            def _():
                near_copy(g).start()

        def add_up_if(kind, *groups):
            @pl.when(adds_other == kind)
            def _():
                for g in groups:
                    add_up(g)

        def wait_rows(g, kind):
            if kind == 0:
                wait_bytes(dist.at[s, g, pl.ds(0, 3 * piece)], ag_rsem.at[s, g, adds_other])
                return

            @pl.when(adds_other == kind)
            def _():
                wait_bytes(dist.at[s, g, pl.ds(0, 3 * piece)], ag_rsem.at[s, g, 0])

            @pl.when(adds_other != kind)
            def _():
                wait_bytes(dist.at[s, g, pl.ds(0, 4 * piece)], ag_rsem.at[s, g, 1])

        def half_copy():
            return copy_to(half_sum.at[s], half_recv.at[s], s_ssem.at[s, 0], s_rsem.at[s, 0], other)

        def scal_copy(i):
            return copy_to(scal.at[s], scal_recv.at[s, i], s_ssem.at[s, 1], s_rsem.at[s, 1], subs[i])

        ring.advance(1)
        ring.hand(1, 7)

        for hf in range(2):
            xo_copy(s, hf).wait_recv()
        jx[own_rows] = hx[s, 0, 0]
        jx[other_rows] = xo[s]
        js = jx[...]
        jh[...], jl[...] = split(-2.0 * js)
        norms_j = jnp.sum(js * js, axis=1, keepdims=True)

        ring.advance(2, (0, 1))
        ring.wait_handed(1, 7)
        gram(0)
        ring.advance(2, (2, 3))
        ring.hand(2, 6)
        ring.advance(3, (0,))
        ring.wait_handed(2, 6)
        gram(1)
        ring.advance(3, (1,))
        add_up_if(1, 0)
        ring.advance(3, (2, 3))
        ring.hand(3, 5)
        if s == 0:
            ring_g.advance(0)
            ring_g.hand(0)
        ring.wait_handed(3, 5)
        gram(2)
        ring.finish()
        add_up_if(1, 1)
        ring.wait_handed(0, 4)
        gram(3)
        whole_sums = [jnp.sum(sums[k], axis=0, keepdims=True) for k in range(2)]
        half_sum[s] = jnp.concatenate([a[:, k * 128 : k * 128 + 128] for a in whole_sums for k in range(4)], axis=0)
        half_copy().start()
        if s == 0:
            ring_g.advance(1)
            ring_g.hand(1, 7)
        add_up_if(1, 2)
        half_copy().wait_recv()
        both = half_sum[s] + half_recv[s]
        scal[s, 0:4] = both[0:4] * both[0:4]
        scal[s, 4:8] = both[4:8]
        for i in range(7):
            scal_copy(i).start()
        if s == 0:
            ring_g.advance(2)
            ring_g.hand(2, 6)
        add_up_if(1, 3)
        add_up_if(0, 0, 1, 2, 3)
        wait_bytes(scal_recv.at[s], s_rsem.at[s, 1])
        both = scal[s]
        for i in range(7):
            both = both + scal_recv[s, i]
        both = jnp.sum(both, axis=1, keepdims=True)
        first_sq = jnp.sum(both[0:4], axis=0, keepdims=True)
        second_all = jnp.sum(both[4:8], axis=0, keepdims=True)
        width = (2.0 * count * second_all - 2.0 * first_sq) / (count * (count - 1.0)) / math.log(count + 1.0)

        whole = pl.ds(0, cols)

        def target(d, e, lanes):
            x, g = hx[s, e, d, :, lanes], hg[e, d, :, lanes]
            if s == 1:
                g = g - cv[0:1, lanes] * (x - hx[0, e, d, :, lanes])
            return 0.5 * width * g - x

        def targets(g):
            t = jnp.concatenate([target(d, e, whole) for d, e in members(g)], axis=0)
            th[g], tl[g] = split(t)

        def weights(g, kind):
            wait_rows(g, kind)
            k = jnp.exp(-dist[s, g, other_rows if kind else own_rows] / width)
            total = jnp.broadcast_to(jnp.sum(k, axis=1, keepdims=True), (rows, 128))
            tot[kind, 128 - rows :] = total if g == 0 else tot[kind, 128 - rows :] + total
            return split(k)

        def pulled(g, kind, k, lanes):
            where = other_rows if kind else own_rows
            result = dot3(k, (th[g, :, lanes], tl[g, :, lanes]), NN)
            pull[s, where, lanes] = result if g == 0 else pull[s, where, lanes] + result

        def p_copy(hf):
            return copy_to(
                pull.at[s, other_rows, lanes_of(hf)], p_recv.at[s, :, lanes_of(hf)], p_ssem.at[s, hf],
                p_rsem.at[s, hf], other,
            )

        def t_copy():
            return copy_to(t_send.at[s], t_recv.at[s], p_ssem.at[s, 2], p_rsem.at[s, 2], other)

        tot[1, 0 : 128 - rows] = jnp.zeros((128 - rows, 128), F32)
        for g in range(4):
            if s == 0:
                ring_g.wait_handed(*GROUPS[g])
            if s == 0 and g == 0:
                ring_g.advance(3)
                ring_g.hand(3, 5)
            if g == 3:
                forward(3)
            targets(g)
            k = weights(g, 1)
            if g < 3:
                pulled(g, 1, k, whole)
                forward(g)
            if s == 0 and g == 1:
                ring_g.advance(4)
                ring_g.hand(4)
        t_send[s] = tot[1].T[0:8]
        t_copy().start()
        for hf in range(2):
            pulled(3, 1, k, lanes_of(hf))
            p_copy(hf).start()
        for g in range(4):
            pulled(g, 0, weights(g, 0), whole)
        t_copy().wait_recv()
        theirs = jnp.broadcast_to(t_recv[s, 0:1], (128, 128)).T[128 - rows :, 0:1]
        total = tot[0, 128 - rows :, 0:1] + theirs
        for hf in range(2):
            lanes = lanes_of(hf)
            p_copy(hf).wait_recv()
            moved = 2.0 * hx[s, 0, 0, :, lanes] + (pull[s, own_rows, lanes] + p_recv[s, :, lanes]) / total
            if s == 0:
                hx[1, 0, 0, :, lanes] = moved
                begin(1, hf)
            else:
                o_ref[:, lanes] = moved
        if s == 0:
            rings[1].hand(0)

        def drain():
            ring.drain()
            for hf in range(2):
                xo_copy(s, hf).wait_send()
                p_copy(hf).wait_send()
            t_copy().wait_send()
            for g in range(4):
                wait_bytes(part.at[s, g, pl.ds(0, 7 * piece)], rs_ssem.at[s, g])

                @pl.when(adds_other == 1)
                def _():
                    wait_bytes(part.at[s, g, pl.ds(0, 7 * piece)], ag_ssem.at[s, g])
                    wait_bytes(part.at[s, g, pl.ds(0, 3 * piece)], fwd_ssem.at[s, g])

                @pl.when(adds_other == 0)
                def _():
                    wait_bytes(part.at[s, g, pl.ds(0, 4 * piece)], ag_ssem.at[s, g])
            half_copy().wait_send()
            wait_bytes(scal_recv.at[s], s_ssem.at[s, 1])

        return drain

    for hf in range(2):
        begin(0, hf)
    rings[0].hand(0)
    drains = [stein(0), stein(1), ring_g.drain]
    for drain in drains:
        drain()


def shards(particles, gradient, curvature):
    rows, cols = particles.shape
    near, far = 2 * rows, 4 * rows
    piece = near // 8
    vmem = pl.BlockSpec(memory_space=pltpu.VMEM)
    dma = pltpu.SemaphoreType.DMA
    return pl.pallas_call(
        kernel,
        name="stein",
        out_shape=jax.ShapeDtypeStruct((rows, cols), F32),
        in_specs=[pl.BlockSpec(memory_space=pltpu.HBM)] * 3,
        out_specs=vmem,
        scratch_shapes=[
            pltpu.VMEM((2, 2, 8, rows, cols), F32),
            pltpu.VMEM((2, 8, rows, cols), F32),
            pltpu.VMEM((1, cols), F32),
            pltpu.VMEM((2, rows, cols), F32),
            pltpu.VMEM((near, cols), F32),
            pltpu.VMEM((near, cols), BF16),
            pltpu.VMEM((near, cols), BF16),
            pltpu.VMEM((2, 4, near, far), F32),
            pltpu.VMEM((2, 4, near, far), F32),
            pltpu.VMEM((2, 4, 7, piece, far), F32),
            pltpu.VMEM((4, far, cols), BF16),
            pltpu.VMEM((4, far, cols), BF16),
            pltpu.VMEM((2, near, cols), F32),
            pltpu.VMEM((2, rows, cols), F32),
            pltpu.VMEM((2, 128, 128), F32),
            pltpu.VMEM((2, 8, 128), F32),
            pltpu.VMEM((2, 8, 128), F32),
            pltpu.VMEM((2, 8, cols), F32),
            pltpu.VMEM((2, 8, 128), F32),
            pltpu.VMEM((2, 8, 128), F32),
            pltpu.VMEM((2, 8, 128), F32),
            pltpu.VMEM((2, 7, 8, 128), F32),
            dma((3, 2, 4)),
            dma((3, 2, 4, CHUNKS)),
            dma((3, 8)),
            dma((3, 8)),
            dma((2, 2)),
            dma((2, 2)),
            dma((2, 4)),
            dma((2, 4)),
            dma((2, 4)),
            dma((2, 4, 2)),
            dma((2, 4)),
            dma((2, 4)),
            dma((2, 2)),
            dma((2, 2)),
            dma((2, 3)),
            dma((2, 3)),
            dma((3,)),
        ],
        compiler_params=pltpu.CompilerParams(
            collective_id=0, has_side_effects=True, vmem_limit_bytes=63 * 2**20 + 2**19
        ),
    )(particles, gradient, curvature.reshape(1, cols))


def solution(mesh):
    in_specs = (P("dom", "sub"), P("dom", "sub"), P("sub"))
    out_specs = P("dom", "sub")
    return jax.shard_map(shards, mesh=mesh, in_specs=in_specs, out_specs=out_specs, check_vma=False)
```
